32 devices in a mesh: seq: 8 (over z, core), ctx: 4 (over y, x).
Axes of the slice: x: 2, y: 2, z: 4, core: 2. Of those that a mesh axis runs over, the one named last changes fastest.
Arguments:
- features: bfloat16 [8, 2048, 2560], P('seq', 'ctx'), may hold values from -6 to 6
- step_sizes: float32 [8, 40, 2048], P('seq', None, 'ctx'), may hold values from 0 to 1, as said below
- rate_logs: float32 [40], replicated, may hold values from -8 to 3
- input_map: bfloat16 [8, 2048, 128], P('seq', 'ctx'), may hold values from -0.5 to 0.5
- output_map: bfloat16 [8, 2048, 128], P('seq', 'ctx'), may hold values from -6 to 6
- skip_gain: float32 [40], replicated, may hold values from 0.5 to 1.5
- state_first: bfloat16 [8, 40, 64, 128], P('seq'), may hold values from -0.5 to 0.5
- upstream: bfloat16 [8, 2048, 2560], P('seq', 'ctx'), may hold values from -45 to 45
- state_last: bfloat16 [8, 40, 64, 128], P('seq'), may hold values from -768 to 768
Outputs:
- grad_features: bfloat16 [8, 2048, 2560], P('seq', 'ctx')
- grad_steps: float32 [8, 40, 2048], P('seq', None, 'ctx')
- grad_input_map: float32 [8, 2048, 128], P('seq', 'ctx')
- grad_output_map: float32 [8, 2048, 128], P('seq', 'ctx')
- grad_rate_logs: float32 [40], replicated
- grad_skip_gain: float32 [40], replicated
The draws below stay inside these ranges and needn't reach their ends.
Inputs may be any that keep to these rules, and one draw needn't show every extreme that they name: `step_sizes`: Positive.
All inputs are finite; a program needn't handle non-finite values.
Results may differ from the reference program's by a relative error of at most 0.0055.
Values sent between devices are 32-bit elements; how exact they have to be, the bound alone decides.
A program may use at most 192 MiB of HBM per device.

```python
import math
from functools import partial
import jax
import jax.numpy as jnp
from jax import lax

H = 40
P_SIZE = 64
N = 128
Q = 256
TOK_DEV = 512
SEQS = 8
TOKENS = 2048


def draw_step_sizes(key, part):
    base_key, factor_key = jax.random.split(key)
    full_shape = (SEQS, H, TOKENS)
    base_steps = jnp.exp(jax.random.uniform(base_key, full_shape, jnp.float32, math.log(0.25), math.log(4.0)))
    factor = jnp.exp(jax.random.uniform(factor_key, (SEQS, H, TOKENS // TOK_DEV), jnp.float32, -math.log(2.0), math.log(2.0)))
    factor = jnp.repeat(factor, TOK_DEV, axis=2)
    return base_steps * factor / math.sqrt(TOKENS)


def draw_rate_logs(key, part):
    order_key, slow_key, quick_key, middle_key = jax.random.split(key, 4)
    shuffled = jax.random.permutation(order_key, H)
    quick_count = max(1, H // 10)
    middle_count = 3 * H // 10
    slow_rate = jnp.exp(jax.random.uniform(slow_key, (H,), jnp.float32, math.log(0.2), math.log(1.4))) / math.sqrt(TOKENS)
    quick_rate = jnp.exp(jax.random.uniform(quick_key, (H,), jnp.float32, math.log(1.0 / 75.0), math.log(1.0 / 45.0))) * math.sqrt(TOKENS)
    middle_rate = jnp.exp(jax.random.uniform(middle_key, (H,), jnp.float32, math.log(0.6), math.log(1.2))) * math.sqrt(TOKENS) / TOK_DEV
    is_quick = shuffled < quick_count
    is_middle = jnp.logical_and(shuffled >= quick_count, shuffled < quick_count + middle_count)
    rates = jnp.where(is_quick, quick_rate, jnp.where(is_middle, middle_rate, slow_rate))
    return jnp.log(rates)


def draw_upstream(key, part):
    noise_key = jax.random.fold_in(key, 0)
    full_shape = (SEQS, TOKENS, H * P_SIZE)
    gaussian = jax.random.truncated_normal(noise_key, -6.0, 6.0, full_shape, jnp.float32)
    sequence_ramp = 1.0 + 2.0 * jnp.arange(SEQS, dtype=jnp.float32) / SEQS
    token_ramp = 1.0 + 2.0 * jnp.arange(TOKENS, dtype=jnp.float32) / TOKENS
    divisor = 3.0
    values = gaussian * sequence_ramp[:, None, None] * token_ramp[None, :, None] / divisor
    return values.astype(jnp.bfloat16)


def level_of(stream_key, extent, pieces, smallest, high):
    def one(dim, parts):
        draws = jax.random.uniform(jax.random.fold_in(jax.random.fold_in(stream_key, 6), dim), (parts,), jnp.float32, smallest / len(pieces), high / len(pieces))
        return jnp.repeat(jnp.exp(draws), extent[dim] // parts).reshape((-1,) + (1,) * (len(extent) - dim - 1))

    level = one(*pieces[0])
    for cut in pieces[1:]:
        level = level * one(*cut)
    return level


def normal_values(stream_key, extent, deviation, most, pieces=(), kind=jnp.bfloat16):
    values = deviation * jax.random.normal(stream_key, extent, jnp.float32)
    if pieces:
        values = values * level_of(stream_key, extent, pieces, -0.22, 0.18)
    return jnp.clip(values, -most, most).astype(kind)


def setup_inputs(seed: int = 0) -> dict:
    seeds = jax.random.split(jax.random.key(seed), 10)
    return {
        "features": normal_values(seeds[0], (SEQS, TOKENS, H * P_SIZE), 1.0, 6.0, ((0, 8), (1, 4))),
        "step_sizes": draw_step_sizes(jax.random.fold_in(seeds[9], 71), 0),
        "rate_logs": draw_rate_logs(jax.random.fold_in(seeds[9], 71), 0),
        "input_map": normal_values(seeds[3], (SEQS, TOKENS, N), N ** -0.5, 0.5, ((0, 8), (1, 4))),
        "output_map": normal_values(seeds[4], (SEQS, TOKENS, N), 1.0, 6.0, ((0, 8), (1, 4))),
        "skip_gain": jnp.clip(jax.random.uniform(seeds[5], (H,), jnp.float32, 0.5, 1.5), 0.5, 1.5),
        "state_first": normal_values(seeds[6], (SEQS, H, P_SIZE, N), N ** -0.5, 0.5, ((0, 8),)),
        "upstream": draw_upstream(jax.random.fold_in(seeds[9], 71), 0),
        "state_last": normal_values(seeds[8], (SEQS, H, P_SIZE, N), (TOK_DEV // 4), 768.0, ((0, 8),)),
    }


def split_blocks(features, step_sizes, input_map, output_map, upstream, head_count):
    length = features.shape[0]
    blocks = length // Q
    head_size = features.shape[1] // head_count
    return (features.reshape(blocks, Q, head_count, head_size),
            jnp.transpose(step_sizes.reshape(head_count, blocks, Q), (1, 0, 2)),
            input_map.reshape(blocks, Q, -1),
            output_map.reshape(blocks, Q, -1),
            upstream.reshape(blocks, Q, head_count, head_size))


def block_local(block_data, decay_rates):
    inputs, steps, map_in, map_out, upstream = block_data
    log_sums = jnp.cumsum(steps * decay_rates[:, None], axis=1)
    end_logs = log_sums[:, Q - 1]
    scaled = jnp.exp(end_logs[:, None] - log_sums) * steps
    decayed_in = (inputs.astype(jnp.float32) * jnp.transpose(scaled)[:, :, None]).astype(jnp.bfloat16)
    decayed_up = (upstream.astype(jnp.float32) * jnp.exp(jnp.transpose(log_sums))[:, :, None]).astype(jnp.bfloat16)
    fresh_block = jnp.einsum("shp,sn->hpn", decayed_in, map_in, preferred_element_type=jnp.float32)
    readout = jnp.einsum("thp,tn->hpn", decayed_up, map_out, preferred_element_type=jnp.float32)
    scores = jnp.dot(map_out, map_in.T, preferred_element_type=jnp.float32)
    inner_dots = jnp.einsum("thp,shp->hts", upstream, inputs, preferred_element_type=jnp.float32)
    causal = jnp.arange(Q)[:, None] >= jnp.arange(Q)[None, :]
    spread = jnp.minimum(log_sums[:, :, None] - log_sums[:, None, :], 0.0)
    kernel = jnp.where(causal[None], jnp.exp(spread), 0.0) * scores[None]
    mixing = (kernel * steps[:, None, :]).astype(jnp.bfloat16)
    grad_inputs = jnp.einsum("hts,thp->shp", mixing, upstream, preferred_element_type=jnp.float32)
    weighted = kernel * inner_dots
    pulled = weighted * steps[:, None, :]
    score_grads = jnp.sum(pulled, axis=0).astype(jnp.bfloat16)
    grad_in = jnp.dot(score_grads.T, map_out, preferred_element_type=jnp.float32)
    grad_out = jnp.dot(score_grads, map_in, preferred_element_type=jnp.float32)
    log_grads = jnp.sum(pulled, axis=2) - jnp.sum(pulled, axis=1)
    step_grads = jnp.sum(weighted, axis=1)
    skip_part = jnp.sum(jnp.diagonal(inner_dots, axis1=1, axis2=2), axis=1)
    return (log_sums, scaled, decayed_in, decayed_up, fresh_block, readout,
            grad_inputs, grad_in, grad_out, log_grads, step_grads, skip_part)


def enter_block(running, element):
    end_log, fresh_block = element
    return jnp.exp(end_log)[:, None, None] * running + fresh_block, running


def finish_block(block_data, decay_rates, skip_gain):
    (inputs, steps, map_in, map_out, upstream, log_sums, scaled, decayed_in, decayed_up,
     entering, leaving, grad_inputs, grad_in, grad_out, log_grads, step_grads) = block_data
    end_logs = log_sums[:, Q - 1]
    entering_half = entering.astype(jnp.bfloat16)
    leaving_half = leaving.astype(jnp.bfloat16)
    carried_out = jnp.einsum("tn,hpn->thp", map_out, entering_half, preferred_element_type=jnp.float32)
    carried_in = jnp.einsum("sn,hpn->shp", map_in, leaving_half, preferred_element_type=jnp.float32)
    upstream_wide = upstream.astype(jnp.float32)
    readout_dots = jnp.transpose(jnp.sum(upstream_wide * carried_out, axis=2))
    input_dots = jnp.transpose(jnp.sum(inputs.astype(jnp.float32) * carried_in, axis=2))
    scaled_rows = jnp.transpose(scaled)[:, :, None]
    features_grad = grad_inputs + scaled_rows * carried_in + skip_gain[None, :, None] * upstream_wide
    in_grad = grad_in + jnp.einsum("shp,hpn->sn", decayed_in, leaving_half, preferred_element_type=jnp.float32)
    out_grad = grad_out + jnp.einsum("thp,hpn->tn", decayed_up, entering_half, preferred_element_type=jnp.float32)
    fresh_terms = scaled * input_dots
    end_extra = jnp.sum(fresh_terms, axis=1) + jnp.exp(end_logs) * jnp.sum(leaving * entering, axis=(1, 2))
    last_token = (jnp.arange(Q) == Q - 1).astype(jnp.float32)
    total_logs = log_grads + jnp.exp(log_sums) * readout_dots - fresh_terms + end_extra[:, None] * last_token[None, :]
    through = jnp.flip(jnp.cumsum(jnp.flip(total_logs, 1), axis=1), 1)
    steps_grad = decay_rates[:, None] * through + step_grads + jnp.exp(end_logs[:, None] - log_sums) * input_dots
    rate_part = jnp.sum(steps * through, axis=1)
    return features_grad, steps_grad, in_grad, out_grad, rate_part


def region_finish(stacked, local_parts, decay_rates, skip_gain, state_in, cot_out):
    end_logs = local_parts[0][:, :, Q - 1]
    _, entering = lax.scan(enter_block, state_in, (end_logs, local_parts[4]))
    _, leaving = lax.scan(enter_block, cot_out, (end_logs, local_parts[5]), reverse=True)
    block_data = stacked + local_parts[:4] + (entering, leaving) + local_parts[6:11]
    return lax.map(partial(finish_block, decay_rates=decay_rates, skip_gain=skip_gain), block_data)


def assemble(finished, local_parts, length, head_count):
    features_grad = finished[0].reshape(length, -1)
    steps_grad = jnp.transpose(finished[1], (1, 0, 2)).reshape(head_count, length)
    in_grad = finished[2].reshape(length, -1)
    out_grad = finished[3].reshape(length, -1)
    rate_sum = jnp.sum(finished[4], axis=0)
    skip_sum = jnp.sum(local_parts[11], axis=0)
    return features_grad, steps_grad, in_grad, out_grad, rate_sum, skip_sum


def sequence_grads(seq_data, decay_rates, skip_gain):
    features, step_sizes, input_map, output_map, state_first, upstream, state_last = seq_data
    head_count = decay_rates.shape[0]
    length = features.shape[0]
    stacked = split_blocks(features, step_sizes, input_map, output_map, upstream, head_count)
    local_parts = lax.map(partial(block_local, decay_rates=decay_rates), stacked)
    finished = region_finish(stacked, local_parts, decay_rates, skip_gain,
                             state_first.astype(jnp.float32), state_last.astype(jnp.float32))
    return assemble(finished, local_parts, length, head_count)


def reference(features, step_sizes, rate_logs, input_map, output_map, skip_gain, state_first, upstream, state_last):
    decay_rates = -jnp.exp(rate_logs)
    results = lax.map(partial(sequence_grads, decay_rates=decay_rates, skip_gain=skip_gain),
                      (features, step_sizes, input_map, output_map, state_first, upstream, state_last))
    return (results[0].astype(jnp.bfloat16), results[1], results[2], results[3],
            decay_rates * jnp.sum(results[4], axis=0), jnp.sum(results[5], axis=0))
```

```python
from functools import partial

import jax
import jax.numpy as jnp
from jax import lax
from jax.experimental import pallas as pl
from jax.experimental.pallas import tpu as pltpu
from jax.sharding import PartitionSpec as P

Q = 256
G = 8
LOG2E = 1.4426950408889634
F32 = jnp.float32
BF16 = jnp.bfloat16
NT = (((1,), (1,)), ((), ()))
TN = (((0,), (0,)), ((), ()))


def fdot(a, b):
    return jnp.dot(a, b, preferred_element_type=F32)


def exact_dot(a, b):
    return jnp.dot(a, b, preferred_element_type=F32, precision=lax.Precision.HIGHEST)


def tri(kind):
    row = lax.broadcasted_iota(jnp.int32, (Q, Q), 0)
    col = lax.broadcasted_iota(jnp.int32, (Q, Q), 1)
    return (row <= col if kind == "prefix" else row >= col).astype(F32)


def states_kernel(size, flags, steps, rates, x, g, bmap, cmap, *outs):
    fresh_out, read_out, ls_out, esum_out, xt_out, gt_out = outs[:6]
    payloads = outs[6:]
    blocks = steps.shape[1] // Q
    prefix = tri("prefix")
    fresh, read, ends = [], [], []
    for c in range(blocks):
        cols = slice(c * Q, (c + 1) * Q)
        step = steps[:, cols]
        logs = exact_dot(step * rates[...], prefix)
        ls_out[:, cols] = logs
        end = logs[:, Q - 1 :]
        scaled = jnp.exp(end - logs) * step
        grown = jnp.exp(logs)
        xt = x[cols, :].T
        gt = g[cols, :].T
        xt_out[:, cols] = xt
        gt_out[:, cols] = gt
        xs, gs = [], []
        for h in range(G):
            rows = slice(h * size, (h + 1) * size)
            xs.append((xt[rows].astype(F32) * scaled[h : h + 1]).astype(BF16))
            gs.append((gt[rows].astype(F32) * grown[h : h + 1]).astype(BF16))
        fresh.append(fdot(jnp.concatenate(xs, 0), bmap[cols, :]))
        read.append(fdot(jnp.concatenate(gs, 0), cmap[cols, :]))
        ends.append(end)
    total = ends[0]
    for c in range(1, blocks):
        fresh_out[c - 1] = fresh[c - 1]
        read_out[c - 1] = read[c]
        total = total + ends[c]
    esum_out[...] = jnp.broadcast_to(total, esum_out.shape)
    for h in range(G):
        rows = slice(h * size, (h + 1) * size)
        state = fresh[0][rows]
        cot = read[-1][rows]
        for c in range(1, blocks):
            state = jnp.exp(ends[c][h : h + 1]) * state + fresh[c][rows]
            back = blocks - 1 - c
            cot = jnp.exp(ends[back][h : h + 1]) * cot + read[back][rows]
        for k, payload in enumerate(payloads):
            payload[rows, :] = jnp.where(flags[k] == 0, state, cot)


def intra_kernel(size, steps, logs, g, xt, gt, bmap, cmap, gf_out, rowsum, colsum, skip,
                 gin, gout, scores, total):
    i = pl.program_id(0)
    blocks = steps.shape[1] // Q
    half = Q // 2

    @pl.when(i == 0)
    def _():
        row = lax.broadcasted_iota(jnp.int32, (Q, Q), 0)
        col = lax.broadcasted_iota(jnp.int32, (Q, Q), 1)
        for c in range(blocks):
            cols = slice(c * Q, (c + 1) * Q)
            s = lax.dot_general(cmap[cols, :], bmap[cols, :], NT, preferred_element_type=F32)
            scores[c] = jnp.where(row >= col, s, 0.0)
        total[...] = jnp.zeros_like(total)

    lane = lax.broadcasted_iota(jnp.int32, (Q, 2 * size), 1)
    for c in range(blocks):
        cols = slice(c * Q, (c + 1) * Q)
        base = c * Q
        lrow = logs[:, cols] * LOG2E
        lcol = lrow.T
        srow = steps[:, cols]
        acc0 = total[c, :half, :half]
        acc1 = total[c, half:, :]
        sums, col_parts, skips = [], [], []
        for h in range(G):
            pair = slice(h // 2 * 2 * size, (h // 2 + 1) * 2 * size)
            rows = slice(h * size, (h + 1) * size)
            mine = lane < size if h % 2 == 0 else lane >= size
            gm = jnp.where(mine, g[cols, pair], jnp.zeros((), BF16))
            row_parts = []
            mixes = []
            column = None
            for slab in range(2):
                ts = slice(slab * half, (slab + 1) * half)
                width = (slab + 1) * half
                ss = slice(0, width)
                inner = fdot(gm[ts], xt[pair, base : base + width])
                spread = jnp.minimum(lcol[ts, h : h + 1] - lrow[h : h + 1, ss], 0.0)
                kern = jnp.exp2(spread) * scores[c, ts, ss]
                step = srow[h : h + 1, ss]
                mixes.append((kern * step).astype(BF16))
                weighted = kern * inner
                pulled = weighted * step
                if slab == 0:
                    acc0 = acc0 + pulled
                else:
                    acc1 = acc1 + pulled
                row_parts.append(jnp.sum(pulled, axis=1, keepdims=True))
                part = jnp.sum(weighted, axis=0, keepdims=True)
                if slab == 0:
                    column = jnp.concatenate([part, jnp.zeros_like(part)], 1)
                else:
                    column = column + part
            col_parts.append(column)
            sums.append(jnp.concatenate(row_parts, 0))
            low = fdot(gt[rows, base : base + half], mixes[0])
            full = fdot(gt[rows, base + half : base + Q], mixes[1])
            gf_out[rows, base : base + half] = low + full[:, :half]
            gf_out[rows, base + half : base + Q] = full[:, half:]
            both = gt[rows, cols].astype(F32) * xt[rows, cols].astype(F32)
            skips.append(jnp.sum(both, axis=0, keepdims=True))
        total[c, :half, :half] = acc0
        total[c, half:, :] = acc1
        colsum[:, cols] = jnp.concatenate(col_parts, 0)
        rowsum[:, cols] = jnp.concatenate(sums, 1).T
        skip[:, cols] = jnp.concatenate(skips, 0)

    @pl.when(i == pl.num_programs(0) - 1)
    def _():
        for c in range(blocks):
            cols = slice(c * Q, (c + 1) * Q)
            grads = total[c].astype(BF16)
            gin[cols, :] = lax.dot_general(grads, cmap[cols, :], TN, preferred_element_type=F32)
            gout[cols, :] = fdot(grads, bmap[cols, :])


def finish_kernel(size, count, weights, gains, steps, rates, logs, rowsum, colsum, skip, xt, gt,
                  gf_in, bmap, cmap, gin, gout, first, last, fresh, read, *rest):
    received = rest[:count]
    gf, gsteps, gin_all, gout_all, rate_part, skip_part, tin, tout = rest[count:]
    i = pl.program_id(0)
    blocks = steps.shape[1] // Q
    suffix = tri("suffix")

    @pl.when(i == 0)
    def _():
        tin[...] = jnp.zeros_like(tin)
        tout[...] = jnp.zeros_like(tout)

    ends = [logs[:, (c + 1) * Q - 1 : (c + 1) * Q] for c in range(blocks)]
    entering = [[None] * G for _ in range(blocks)]
    leaving = [[None] * G for _ in range(blocks)]
    for h in range(G):
        head = i * G + h
        rows = slice(h * size, (h + 1) * size)
        state = weights[0, 0, head] * first[rows].astype(F32)
        cot = weights[1, 0, head] * last[rows].astype(F32)
        for d in range(count):
            value = received[d][rows]
            state = state + weights[0, d + 1, head] * value
            cot = cot + weights[1, d + 1, head] * value
        entering[0][h] = state
        leaving[-1][h] = cot
        for c in range(1, blocks):
            entering[c][h] = jnp.exp(ends[c - 1][h : h + 1]) * entering[c - 1][h] + fresh[c - 1, rows]
            b = blocks - 1 - c
            leaving[b][h] = jnp.exp(ends[b + 1][h : h + 1]) * leaving[b + 1][h] + read[b, rows]
    rate_total = jnp.zeros((G, 1), F32)
    lane = lax.broadcasted_iota(jnp.int32, (1, Q), 1)
    for c in range(blocks):
        cols = slice(c * Q, (c + 1) * Q)
        log = logs[:, cols]
        step = steps[:, cols]
        decay = jnp.exp(ends[c] - log)
        scaled = decay * step
        grown = jnp.exp(log)
        eb = jnp.concatenate([e.astype(BF16) for e in entering[c]], 0)
        lb = jnp.concatenate([e.astype(BF16) for e in leaving[c]], 0)
        out_t = lax.dot_general(eb, cmap[cols, :], NT, preferred_element_type=F32)
        in_t = lax.dot_general(lb, bmap[cols, :], NT, preferred_element_type=F32)
        xs, gs, rdots, idots, prods = [], [], [], [], []
        for h in range(G):
            rows = slice(h * size, (h + 1) * size)
            xh = xt[rows, cols].astype(F32)
            gh = gt[rows, cols].astype(F32)
            sc = scaled[h : h + 1]
            xs.append((xh * sc).astype(BF16))
            gs.append((gh * grown[h : h + 1]).astype(BF16))
            rdots.append(jnp.sum(gh * out_t[rows], axis=0, keepdims=True))
            idots.append(jnp.sum(xh * in_t[rows], axis=0, keepdims=True))
            prods.append(jnp.sum(leaving[c][h] * entering[c][h], axis=0, keepdims=True))
            grad = gf_in[rows, cols] + sc * in_t[rows] + gains[i * G + h] * gh
            gf[cols, rows] = grad.T.astype(BF16)
        tin[:, cols] += lax.dot_general(lb, jnp.concatenate(xs, 0), TN, preferred_element_type=F32)
        tout[:, cols] += lax.dot_general(eb, jnp.concatenate(gs, 0), TN, preferred_element_type=F32)
        rdot = jnp.concatenate(rdots, 0)
        idot = jnp.concatenate(idots, 0)
        prod = jnp.sum(jnp.concatenate(prods, 0), axis=1, keepdims=True)
        terms = scaled * idot
        extra = jnp.sum(terms, axis=1, keepdims=True) + jnp.exp(ends[c]) * prod
        weighted = colsum[:, cols]
        logs_grad = rowsum[:, cols] - step * weighted + grown * rdot - terms
        logs_grad = logs_grad + jnp.where(lane == Q - 1, extra, 0.0)
        through = exact_dot(logs_grad, suffix)
        gsteps[:, cols] = rates[...] * through + weighted + decay * idot
        rate_total = rate_total + jnp.sum(step * through, axis=1, keepdims=True)
    rate_part[...] = rates[...] * rate_total
    skip_part[...] = jnp.sum(skip[...], axis=1, keepdims=True)

    @pl.when(i == pl.num_programs(0) - 1)
    def _():
        gin_all[...] = gin[...] + tin[...].T
        gout_all[...] = gout[...] + tout[...].T


def local(features, step_sizes, rate_logs, input_map, output_map, skip_gain, state_first,
          upstream, state_last):
    heads = rate_logs.shape[0]
    length = features.shape[1]
    size = features.shape[2] // heads
    dim = input_map.shape[2]
    blocks = length // Q
    x, g, steps = features[0], upstream[0], step_sizes[0]
    bmap, cmap = input_map[0], output_map[0]
    rates = -jnp.exp(rate_logs)[:, None]
    n = lax.axis_size("ctx")
    me = lax.axis_index("ctx")
    levels = n.bit_length() - 1
    flags = (me >> jnp.arange(max(levels, 1))) & 1
    wide = G * size
    grid = (heads // G,)
    params = pltpu.CompilerParams(vmem_limit_bytes=56 * 1024 * 1024)
    smem = pl.BlockSpec(memory_space=pltpu.SMEM)
    head_rows = pl.BlockSpec((G, length), lambda i: (i, 0))
    rate_rows = pl.BlockSpec((G, 1), lambda i: (i, 0))
    natural = pl.BlockSpec((length, wide), lambda i: (0, i))
    turned = pl.BlockSpec((wide, length), lambda i: (i, 0))
    whole = pl.BlockSpec((length, dim), lambda i: (0, 0))
    state = pl.BlockSpec((wide, dim), lambda i: (i, 0))
    inner = pl.BlockSpec((blocks - 1, wide, dim), lambda i: (0, i, 0))
    state_shape = jax.ShapeDtypeStruct((heads * size, dim), F32)
    inner_shape = jax.ShapeDtypeStruct((blocks - 1, heads * size, dim), F32)
    row_shape = jax.ShapeDtypeStruct((heads, length), F32)
    map_shape = jax.ShapeDtypeStruct((length, dim), F32)
    one_shape = jax.ShapeDtypeStruct((heads, 1), F32)
    turned_shape = jax.ShapeDtypeStruct((heads * size, length), BF16)
    fresh, read, logs, esum, xt, gt, *payloads = pl.pallas_call(
        partial(states_kernel, size),
        grid=grid,
        in_specs=[smem, head_rows, rate_rows, natural, natural, whole, whole],
        out_specs=[inner, inner, head_rows, rate_rows, turned, turned] + [state] * levels,
        out_shape=[inner_shape, inner_shape, row_shape, one_shape, turned_shape, turned_shape]
        + [state_shape] * levels,
        compiler_params=params,
        name="states",
        cost_estimate=pl.CostEstimate(flops=10**9, bytes_accessed=14 * 10**6, transcendentals=0),
    )(flags, steps, rates, x, g, bmap, cmap)

    received, sums = [], []
    for d in range(1, n):
        pairs = [(i, i ^ d) for i in range(n)]
        received.append(lax.ppermute(payloads[d.bit_length() - 1], "ctx", pairs))
        sums.append(lax.ppermute(esum, "ctx", pairs))

    gf_in, rowsum, colsum, skip, gin, gout = pl.pallas_call(
        partial(intra_kernel, size),
        grid=grid,
        in_specs=[head_rows, head_rows, natural, turned, turned, whole, whole],
        out_specs=[turned, head_rows, head_rows, head_rows, whole, whole],
        out_shape=[jax.ShapeDtypeStruct((heads * size, length), F32), row_shape, row_shape,
                   row_shape, map_shape, map_shape],
        scratch_shapes=[pltpu.VMEM((blocks, Q, Q), F32)] * 2,
        compiler_params=params,
        name="intra",
        cost_estimate=pl.CostEstimate(flops=2 * 10**10, bytes_accessed=16 * 10**6,
                                      transcendentals=0),
    )(steps, logs, g, xt, gt, bmap, cmap)

    others = jnp.arange(n)
    by_distance = jnp.stack([esum[:, 0]] + [s[:, 0] for s in sums])
    by_place = by_distance[others ^ me]
    source = (me ^ others)[:, None]
    between = others[None, :]
    ahead = (source < between) & (between < me)
    behind = (me < between) & (between < source)
    fore = jnp.where(source < me, jnp.exp(jnp.where(ahead[:, :, None], by_place[None], 0.0).sum(1)), 0.0)
    aft = jnp.where(source > me, jnp.exp(jnp.where(behind[:, :, None], by_place[None], 0.0).sum(1)), 0.0)
    enter = jnp.exp(jnp.where((others < me)[:, None], by_place, 0.0).sum(0))
    leave = jnp.exp(jnp.where((others > me)[:, None], by_place, 0.0).sum(0))
    weights = jnp.stack([fore.at[0].set(enter), aft.at[0].set(leave)])

    gf, gsteps, gin, gout, rate_part, skip_part = pl.pallas_call(
        partial(finish_kernel, size, n - 1),
        grid=grid,
        in_specs=[smem, smem, head_rows, rate_rows, head_rows, head_rows, head_rows, head_rows,
                  turned, turned, turned, whole, whole, whole, whole, state, state, inner, inner]
        + [state] * (n - 1),
        out_specs=[natural, head_rows, whole, whole, rate_rows, rate_rows],
        out_shape=[jax.ShapeDtypeStruct((length, heads * size), BF16), row_shape, map_shape,
                   map_shape, one_shape, one_shape],
        scratch_shapes=[pltpu.VMEM((dim, length), F32)] * 2,
        compiler_params=params,
        name="finish",
        cost_estimate=pl.CostEstimate(flops=2 * 10**9, bytes_accessed=30 * 10**6,
                                      transcendentals=0),
    )(weights, skip_gain, steps, rates, logs, rowsum, colsum, skip, xt, gt, gf_in, bmap, cmap,
      gin, gout, state_first[0].reshape(heads * size, dim), state_last[0].reshape(heads * size, dim),
      fresh, read, *received)
    sums = lax.psum(jnp.concatenate([rate_part[:, 0], skip_part[:, 0]]), ("ctx", "seq"))
    return (gf[None], gsteps[None], gin[None], gout[None], sums[:heads], sums[heads:])


def solution(mesh):
    tokens = P("seq", "ctx", None)
    state = P("seq", None, None, None)
    head_tokens = P("seq", None, "ctx")
    return jax.shard_map(
        local,
        mesh=mesh,
        in_specs=(tokens, head_tokens, P(), tokens, tokens, P(), state, tokens, state),
        out_specs=(tokens, head_tokens, tokens, tokens, P(), P()),
        check_vma=False,
    )
```

```python
from functools import partial

import jax
import jax.numpy as jnp
from jax import lax
from jax.experimental import pallas as pl
from jax.experimental.pallas import tpu as pltpu
from jax.sharding import PartitionSpec as P

Q = 256
G = 8
LOG2E = 1.4426950408889634
F32 = jnp.float32
BF16 = jnp.bfloat16
NT = (((1,), (1,)), ((), ()))
TN = (((0,), (0,)), ((), ()))


def fdot(a, b):
    return jnp.dot(a, b, preferred_element_type=F32)


def exact_dot(a, b):
    return jnp.dot(a, b, preferred_element_type=F32, precision=lax.Precision.HIGHEST)


def tri(kind):
    row = lax.broadcasted_iota(jnp.int32, (Q, Q), 0)
    col = lax.broadcasted_iota(jnp.int32, (Q, Q), 1)
    return (row <= col if kind == "prefix" else row >= col).astype(F32)


def states_kernel(size, held, flags, steps, rates, x, g, bmap, cmap, *rest):
    ls_out, xt_out, gt_out, fresh_out, read_out = rest[held : held + 5]
    payloads = rest[held + 5 :]
    blocks = steps.shape[1] // Q
    prefix = tri("prefix")
    fresh, read, ends = [], [], []
    for c in range(blocks):
        cols = slice(c * Q, (c + 1) * Q)
        step = steps[:, cols]
        logs = exact_dot(step * rates[...], prefix)
        ls_out[:, cols] = logs
        end = logs[:, Q - 1 :]
        scaled = jnp.exp(end - logs) * step
        grown = jnp.exp(logs)
        xt = x[cols, :].T
        gt = g[cols, :].T
        xt_out[:, cols] = xt
        gt_out[:, cols] = gt
        xs, gs = [], []
        for h in range(G):
            rows = slice(h * size, (h + 1) * size)
            xs.append((xt[rows].astype(F32) * scaled[h : h + 1]).astype(BF16))
            gs.append((gt[rows].astype(F32) * grown[h : h + 1]).astype(BF16))
        fresh.append(fdot(jnp.concatenate(xs, 0), bmap[cols, :]))
        read.append(fdot(jnp.concatenate(gs, 0), cmap[cols, :]))
        ends.append(end)
    for c in range(1, blocks):
        fresh_out[c - 1] = fresh[c - 1]
        read_out[c - 1] = read[c]
    for h in range(G):
        rows = slice(h * size, (h + 1) * size)
        state = fresh[0][rows]
        cot = read[-1][rows]
        for c in range(1, blocks):
            state = jnp.exp(ends[c][h : h + 1]) * state + fresh[c][rows]
            back = blocks - 1 - c
            cot = jnp.exp(ends[back][h : h + 1]) * cot + read[back][rows]
        for k, payload in enumerate(payloads):
            payload[rows, :] = jnp.where(flags[k] == 0, state, cot)


def intra_kernel(size, steps, logs, g, xt, gt, bmap, cmap, gf_out, rowsum, colsum, skip,
                 gin, gout, scores, total):
    i = pl.program_id(0)
    blocks = steps.shape[1] // Q
    half = Q // 2

    @pl.when(i == 0)
    def _():
        row = lax.broadcasted_iota(jnp.int32, (Q, Q), 0)
        col = lax.broadcasted_iota(jnp.int32, (Q, Q), 1)
        for c in range(blocks):
            cols = slice(c * Q, (c + 1) * Q)
            s = lax.dot_general(cmap[cols, :], bmap[cols, :], NT, preferred_element_type=F32)
            scores[c] = jnp.where(row >= col, s, 0.0)
        total[...] = jnp.zeros_like(total)

    lane = lax.broadcasted_iota(jnp.int32, (Q, 2 * size), 1)
    for c in range(blocks):
        cols = slice(c * Q, (c + 1) * Q)
        base = c * Q
        lrow = logs[:, cols] * LOG2E
        lcol = lrow.T
        srow = steps[:, cols]
        acc0 = total[c, :half, :half]
        acc1 = total[c, half:, :]
        sums, col_parts, skips = [], [], []
        for h in range(G):
            pair = slice(h // 2 * 2 * size, (h // 2 + 1) * 2 * size)
            rows = slice(h * size, (h + 1) * size)
            mine = lane < size if h % 2 == 0 else lane >= size
            gm = jnp.where(mine, g[cols, pair], jnp.zeros((), BF16))
            row_parts = []
            mixes = []
            column = None
            for slab in range(2):
                ts = slice(slab * half, (slab + 1) * half)
                width = (slab + 1) * half
                ss = slice(0, width)
                inner = fdot(gm[ts], xt[pair, base : base + width])
                spread = jnp.minimum(lcol[ts, h : h + 1] - lrow[h : h + 1, ss], 0.0)
                kern = jnp.exp2(spread) * scores[c, ts, ss]
                step = srow[h : h + 1, ss]
                mixes.append((kern * step).astype(BF16))
                weighted = kern * inner
                pulled = weighted * step
                if slab == 0:
                    acc0 = acc0 + pulled
                else:
                    acc1 = acc1 + pulled
                row_parts.append(jnp.sum(pulled, axis=1, keepdims=True))
                part = jnp.sum(weighted, axis=0, keepdims=True)
                if slab == 0:
                    column = jnp.concatenate([part, jnp.zeros_like(part)], 1)
                else:
                    column = column + part
            col_parts.append(column)
            sums.append(jnp.concatenate(row_parts, 0))
            low = fdot(gt[rows, base : base + half], mixes[0])
            full = fdot(gt[rows, base + half : base + Q], mixes[1])
            gf_out[rows, base : base + half] = low + full[:, :half]
            gf_out[rows, base + half : base + Q] = full[:, half:]
            both = gt[rows, cols].astype(F32) * xt[rows, cols].astype(F32)
            skips.append(jnp.sum(both, axis=0, keepdims=True))
        total[c, :half, :half] = acc0
        total[c, half:, :] = acc1
        colsum[:, cols] = jnp.concatenate(col_parts, 0)
        rowsum[:, cols] = jnp.concatenate(sums, 1).T
        skip[:, cols] = jnp.concatenate(skips, 0)

    @pl.when(i == pl.num_programs(0) - 1)
    def _():
        for c in range(blocks):
            cols = slice(c * Q, (c + 1) * Q)
            grads = total[c].astype(BF16)
            gin[cols, :] = lax.dot_general(grads, cmap[cols, :], TN, preferred_element_type=F32)
            gout[cols, :] = fdot(grads, bmap[cols, :])


def finish_kernel(size, count, base, held, weights, gains, steps, rates, logs, rowsum, colsum, skip, xt, gt,
                  gf_in, bmap, cmap, gin, gout, first, last, fresh, read, *rest):
    received = rest[:count]
    gf, gsteps, gin_all, gout_all, rate_part, skip_part, tin, tout = rest[count + held :]
    i = pl.program_id(0)
    blocks = steps.shape[1] // Q
    suffix = tri("suffix")

    @pl.when(i == 0)
    def _():
        tin[...] = jnp.zeros_like(tin)
        tout[...] = jnp.zeros_like(tout)

    ends = [logs[:, (c + 1) * Q - 1 : (c + 1) * Q] for c in range(blocks)]
    entering = [[None] * G for _ in range(blocks)]
    leaving = [[None] * G for _ in range(blocks)]
    for h in range(G):
        head = (base + i) * G + h
        rows = slice(h * size, (h + 1) * size)
        state = weights[0, 0, head] * first[rows].astype(F32)
        cot = weights[1, 0, head] * last[rows].astype(F32)
        for d in range(count):
            value = received[d][rows]
            state = state + weights[0, d + 1, head] * value
            cot = cot + weights[1, d + 1, head] * value
        entering[0][h] = state
        leaving[-1][h] = cot
        for c in range(1, blocks):
            entering[c][h] = jnp.exp(ends[c - 1][h : h + 1]) * entering[c - 1][h] + fresh[c - 1, rows]
            b = blocks - 1 - c
            leaving[b][h] = jnp.exp(ends[b + 1][h : h + 1]) * leaving[b + 1][h] + read[b, rows]
    rate_total = jnp.zeros((G, 1), F32)
    lane = lax.broadcasted_iota(jnp.int32, (1, Q), 1)
    for c in range(blocks):
        cols = slice(c * Q, (c + 1) * Q)
        log = logs[:, cols]
        step = steps[:, cols]
        decay = jnp.exp(ends[c] - log)
        scaled = decay * step
        grown = jnp.exp(log)
        eb = jnp.concatenate([e.astype(BF16) for e in entering[c]], 0)
        lb = jnp.concatenate([e.astype(BF16) for e in leaving[c]], 0)
        out_t = lax.dot_general(eb, cmap[cols, :], NT, preferred_element_type=F32)
        in_t = lax.dot_general(lb, bmap[cols, :], NT, preferred_element_type=F32)
        xs, gs, rdots, idots, prods = [], [], [], [], []
        for h in range(G):
            rows = slice(h * size, (h + 1) * size)
            xh = xt[rows, cols].astype(F32)
            gh = gt[rows, cols].astype(F32)
            sc = scaled[h : h + 1]
            xs.append((xh * sc).astype(BF16))
            gs.append((gh * grown[h : h + 1]).astype(BF16))
            rdots.append(jnp.sum(gh * out_t[rows], axis=0, keepdims=True))
            idots.append(jnp.sum(xh * in_t[rows], axis=0, keepdims=True))
            prods.append(jnp.sum(leaving[c][h] * entering[c][h], axis=0, keepdims=True))
            grad = gf_in[rows, cols] + sc * in_t[rows] + gains[(base + i) * G + h] * gh
            gf[cols, rows] = grad.T.astype(BF16)
        tin[:, cols] += lax.dot_general(lb, jnp.concatenate(xs, 0), TN, preferred_element_type=F32)
        tout[:, cols] += lax.dot_general(eb, jnp.concatenate(gs, 0), TN, preferred_element_type=F32)
        rdot = jnp.concatenate(rdots, 0)
        idot = jnp.concatenate(idots, 0)
        prod = jnp.sum(jnp.concatenate(prods, 0), axis=1, keepdims=True)
        terms = scaled * idot
        extra = jnp.sum(terms, axis=1, keepdims=True) + jnp.exp(ends[c]) * prod
        weighted = colsum[:, cols]
        logs_grad = rowsum[:, cols] - step * weighted + grown * rdot - terms
        logs_grad = logs_grad + jnp.where(lane == Q - 1, extra, 0.0)
        through = exact_dot(logs_grad, suffix)
        gsteps[:, cols] = rates[...] * through + weighted + decay * idot
        rate_total = rate_total + jnp.sum(step * through, axis=1, keepdims=True)
    rate_part[...] = rates[...] * rate_total
    skip_part[...] = jnp.sum(skip[...], axis=1, keepdims=True)

    @pl.when(i == pl.num_programs(0) - 1)
    def _():
        gin_all[...] = gin[...] + tin[...].T
        gout_all[...] = gout[...] + tout[...].T


def sums_kernel(n, m, parts, *refs):
    rates, skips = refs[:parts], refs[parts : 2 * parts]
    out, mine, first, second, send1, recv1, send2, recv2 = refs[2 * parts :]
    here, there = lax.axis_index("ctx"), lax.axis_index("seq")
    barrier = pltpu.get_barrier_semaphore()
    for d in range(1, n):
        pl.semaphore_signal(barrier, inc=1, device_id={"ctx": lax.rem(here + d, n)},
                            device_id_type=pl.DeviceIdType.MESH)
    for d in range(1, m):
        pl.semaphore_signal(barrier, inc=1, device_id={"seq": lax.rem(there + d, m)},
                            device_id_type=pl.DeviceIdType.MESH)
    heads = out.shape[1]
    row = lax.broadcasted_iota(jnp.int32, (heads, heads), 0)
    col = lax.broadcasted_iota(jnp.int32, (heads, heads), 1)
    mine[...] = jnp.zeros_like(mine)
    for k, group in enumerate((rates, skips)):
        column = jnp.concatenate([r[...] for r in group], 0)
        line = jnp.sum(jnp.where(row == col, column, 0.0), axis=0, keepdims=True)
        mine[k : k + 1, :heads] = line
    pl.semaphore_wait(barrier, n + m - 2)

    def exchange(axis, place, count, slots, send, recv):
        copies = []
        slots[place] = mine[...]
        for d in range(1, count):
            copy = pltpu.make_async_remote_copy(
                src_ref=mine, dst_ref=slots.at[place], send_sem=send.at[d],
                recv_sem=recv.at[place], device_id={axis: lax.rem(place + d, count)},
                device_id_type=pl.DeviceIdType.MESH)
            copy.start()
            copies.append(copy)
        for d in range(1, count):
            source = lax.rem(place + count - d, count)
            pltpu.make_async_remote_copy(
                src_ref=mine, dst_ref=slots.at[source], send_sem=send.at[d],
                recv_sem=recv.at[source], device_id={axis: source},
                device_id_type=pl.DeviceIdType.MESH).wait_recv()
        for copy in copies:
            copy.wait_send()
        total = slots[0]
        for k in range(1, count):
            total = total + slots[k]
        return total

    mine[...] = exchange("ctx", here, n, first, send1, recv1)
    out[...] = exchange("seq", there, m, second, send2, recv2)[:2, :heads]


def local(features, step_sizes, rate_logs, input_map, output_map, skip_gain, state_first,
          upstream, state_last):
    heads = rate_logs.shape[0]
    length = features.shape[1]
    size = features.shape[2] // heads
    dim = input_map.shape[2]
    blocks = length // Q
    x, g, steps = features[0], upstream[0], step_sizes[0]
    bmap, cmap = input_map[0], output_map[0]
    first = state_first[0].reshape(heads * size, dim)
    last = state_last[0].reshape(heads * size, dim)
    rates = -jnp.exp(rate_logs)[:, None]
    n, m = lax.axis_size("ctx"), lax.axis_size("seq")
    me = lax.axis_index("ctx")
    levels = n.bit_length() - 1
    flags = (me >> jnp.arange(max(levels, 1))) & 1
    wide = G * size
    groups = heads // G
    chunks = [(0, groups)]
    params = pltpu.CompilerParams(vmem_limit_bytes=56 * 1024 * 1024)
    smem = pl.BlockSpec(memory_space=pltpu.SMEM)
    anywhere = pl.BlockSpec(memory_space=pl.ANY)
    whole = pl.BlockSpec((length, dim), lambda i: (0, 0))

    def specs(base):
        return (
            pl.BlockSpec((G, length), lambda i: (base + i, 0)),
            pl.BlockSpec((G, 1), lambda i: (base + i, 0)),
            pl.BlockSpec((length, wide), lambda i: (0, base + i)),
            pl.BlockSpec((wide, length), lambda i: (base + i, 0)),
            pl.BlockSpec((wide, dim), lambda i: (base + i, 0)),
            pl.BlockSpec((blocks - 1, wide, dim), lambda i: (0, base + i, 0)),
        )

    head_rows0, rate_rows0, natural0, turned0, state0, inner0 = specs(0)
    row_shape = jax.ShapeDtypeStruct((heads, length), F32)
    map_shape = jax.ShapeDtypeStruct((length, dim), F32)
    turned_shape = jax.ShapeDtypeStruct((heads * size, length), BF16)

    esum = jnp.sum(steps, axis=1, keepdims=True) * rates
    pairs = [[(i, i ^ d) for i in range(n)] for d in range(n)]
    sums = [lax.ppermute(esum, "ctx", pairs[d]) for d in range(1, n)]

    shared, states = (), []
    for base, width in chunks:
        head_rows, rate_rows, natural, turned, state, inner = specs(base)
        held = len(shared)
        inner_shape = jax.ShapeDtypeStruct((blocks - 1, width * wide, dim), F32)
        *shared, fresh, read = results = pl.pallas_call(
            partial(states_kernel, size, held),
            grid=(width,),
            in_specs=[smem, head_rows, rate_rows, natural, natural, whole, whole]
            + [anywhere] * held,
            out_specs=[head_rows, turned, turned, inner0, inner0] + [state0] * levels,
            out_shape=[row_shape, turned_shape, turned_shape, inner_shape, inner_shape]
            + [jax.ShapeDtypeStruct((width * wide, dim), F32)] * levels,
            input_output_aliases={7 + k: k for k in range(held)},
            compiler_params=params,
            name="states",
            cost_estimate=pl.CostEstimate(flops=2 * 10**8 * width,
                                          bytes_accessed=3 * 10**6 * width, transcendentals=0),
        )(flags, steps, rates, x, g, bmap, cmap, *shared)
        shared, fresh, read, payloads = results[:3], results[3], results[4], results[5:]
        received = [lax.ppermute(payloads[d.bit_length() - 1], "ctx", pairs[d])
                    for d in range(1, n)]
        states.append((fresh, read, received))
    logs, xt, gt = shared

    gf_in, rowsum, colsum, skip, gin, gout = pl.pallas_call(
        partial(intra_kernel, size),
        grid=(groups,),
        in_specs=[head_rows0, head_rows0, natural0, turned0, turned0, whole, whole],
        out_specs=[turned0, head_rows0, head_rows0, head_rows0, whole, whole],
        out_shape=[jax.ShapeDtypeStruct((heads * size, length), F32), row_shape, row_shape,
                   row_shape, map_shape, map_shape],
        scratch_shapes=[pltpu.VMEM((blocks, Q, Q), F32)] * 2,
        compiler_params=params,
        name="intra",
        cost_estimate=pl.CostEstimate(flops=2 * 10**10, bytes_accessed=16 * 10**6,
                                      transcendentals=0),
    )(steps, logs, g, xt, gt, bmap, cmap)

    others = jnp.arange(n)
    by_distance = jnp.stack([esum[:, 0]] + [s[:, 0] for s in sums])
    by_place = by_distance[others ^ me]
    source = (me ^ others)[:, None]
    between = others[None, :]
    ahead = (source < between) & (between < me)
    behind = (me < between) & (between < source)
    fore = jnp.where(source < me, jnp.exp(jnp.where(ahead[:, :, None], by_place[None], 0.0).sum(1)), 0.0)
    aft = jnp.where(source > me, jnp.exp(jnp.where(behind[:, :, None], by_place[None], 0.0).sum(1)), 0.0)
    enter = jnp.exp(jnp.where((others < me)[:, None], by_place, 0.0).sum(0))
    leave = jnp.exp(jnp.where((others > me)[:, None], by_place, 0.0).sum(0))
    weights = jnp.stack([fore.at[0].set(enter), aft.at[0].set(leave)])

    grads, rate_parts, skip_parts = (), [], []
    for (base, width), (fresh, read, received) in zip(chunks, states):
        head_rows, rate_rows, natural, turned, state, inner = specs(base)
        held = len(grads)
        one_shape = jax.ShapeDtypeStruct((width * G, 1), F32)
        *grads, gin, gout, rate_part, skip_part = pl.pallas_call(
            partial(finish_kernel, size, n - 1, base, held),
            grid=(width,),
            in_specs=[smem, smem, head_rows, rate_rows, head_rows, head_rows, head_rows,
                      head_rows, turned, turned, turned, whole, whole, whole, whole, state, state,
                      inner0, inner0] + [state0] * (n - 1) + [anywhere] * held,
            out_specs=[natural, head_rows, whole, whole, rate_rows0, rate_rows0],
            out_shape=[jax.ShapeDtypeStruct((length, heads * size), BF16), row_shape, map_shape,
                       map_shape, one_shape, one_shape],
            scratch_shapes=[pltpu.VMEM((dim, length), F32)] * 2,
            input_output_aliases={18 + n + k: k for k in range(held)},
            compiler_params=params,
            name="finish",
            cost_estimate=pl.CostEstimate(flops=4 * 10**8 * width,
                                          bytes_accessed=6 * 10**6 * width, transcendentals=0),
        )(weights, skip_gain, steps, rates, logs, rowsum, colsum, skip, xt, gt, gf_in, bmap, cmap,
          gin, gout, first, last, fresh, read, *received, *grads)
        rate_parts.append(rate_part)
        skip_parts.append(skip_part)
    gf, gsteps = grads

    lanes = -(-heads // 128) * 128
    vmem = pl.BlockSpec(memory_space=pltpu.VMEM)
    dma = pltpu.SemaphoreType.DMA
    totals = pl.pallas_call(
        partial(sums_kernel, n, m, len(chunks)),
        in_specs=[vmem] * (2 * len(chunks)),
        out_specs=vmem,
        out_shape=jax.ShapeDtypeStruct((2, heads), F32),
        scratch_shapes=[pltpu.VMEM((8, lanes), F32), pltpu.VMEM((n, 8, lanes), F32),
                        pltpu.VMEM((m, 8, lanes), F32), dma((n,)), dma((n,)), dma((m,)),
                        dma((m,))],
        compiler_params=pltpu.CompilerParams(collective_id=0, has_side_effects=True),
        name="sums",
    )(*rate_parts, *skip_parts)
    return (gf[None], gsteps[None], gin[None], gout[None], totals[0], totals[1])


def solution(mesh):
    tokens = P("seq", "ctx", None)
    state = P("seq", None, None, None)
    head_tokens = P("seq", None, "ctx")
    return jax.shard_map(
        local,
        mesh=mesh,
        in_specs=(tokens, head_tokens, P(), tokens, tokens, P(), state, tokens, state),
        out_specs=(tokens, head_tokens, tokens, tokens, P(), P()),
        check_vma=False,
    )
```

```python
from functools import partial

import jax
import jax.numpy as jnp
from jax import lax
from jax.experimental import pallas as pl
from jax.experimental.pallas import tpu as pltpu
from jax.sharding import PartitionSpec as P

Q = 256
G = 8
LOG2E = 1.4426950408889634
F32 = jnp.float32
BF16 = jnp.bfloat16
NT = (((1,), (1,)), ((), ()))
TN = (((0,), (0,)), ((), ()))


def fdot(a, b):
    return jnp.dot(a, b, preferred_element_type=F32)


def exact_dot(a, b):
    return jnp.dot(a, b, preferred_element_type=F32, precision=lax.Precision.HIGHEST)


def tri(kind):
    row = lax.broadcasted_iota(jnp.int32, (Q, Q), 0)
    col = lax.broadcasted_iota(jnp.int32, (Q, Q), 1)
    return (row <= col if kind == "prefix" else row >= col).astype(F32)


def partner(place, distance):
    other = place
    for k in range(distance.bit_length()):
        if distance >> k & 1:
            other = other + (1 - 2 * (place // 2**k % 2)) * 2**k
    return other


def local_kernel(size, n, steps, rates, x, g, bmap, cmap, *refs):
    ls_out, xt_out, gt_out, fresh_out, read_out = refs[:5]
    gf_out, rowsum, colsum, skip, gin, gout = refs[5:11]
    received = refs[11 : 10 + n]
    scores, total, logs, xts, gts, sent, send_sem, recv_sem = refs[10 + n :]
    i = pl.program_id(0)
    groups = pl.num_programs(0) // 2
    me = lax.axis_index("ctx")

    def copy(d, group):
        return pltpu.make_async_remote_copy(
            src_ref=sent.at[group, d.bit_length() - 1], dst_ref=received[d - 1].at[group],
            send_sem=send_sem.at[d - 1, group], recv_sem=recv_sem.at[d - 1, group],
            device_id={"ctx": partner(me, d)}, device_id_type=pl.DeviceIdType.MESH)

    @pl.when(i == 0)
    def _():
        barrier = pltpu.get_barrier_semaphore()
        for d in range(1, n):
            pl.semaphore_signal(barrier, inc=1, device_id={"ctx": partner(me, d)},
                                device_id_type=pl.DeviceIdType.MESH)
        pl.semaphore_wait(barrier, n - 1)

    @pl.when(i < groups)
    def _():
        states_step(size, n, me, steps, rates, x, g, bmap, cmap, ls_out, xt_out, gt_out,
                    fresh_out, read_out, logs.at[i], xts.at[i], gts.at[i], sent.at[i])
        for d in range(1, n):
            copy(d, i).start()

    @pl.when(i >= groups)
    def _():
        k = i - groups
        intra_step(size, k, groups, steps, logs.at[k], g, xts.at[k], gts.at[k], bmap, cmap,
                   gf_out, rowsum, colsum, skip, gin, gout, scores, total)

    @pl.when(i == 2 * groups - 1)
    def _():
        for group in range(sent.shape[0]):
            for d in range(1, n):
                copy(d, group).wait()


def states_step(size, n, me, steps, rates, x, g, bmap, cmap, ls_out, xt_out, gt_out, fresh_out,
                read_out, logs_held, xt_held, gt_held, sent):
    blocks = steps.shape[1] // Q
    prefix = tri("prefix")
    fresh, read, ends = [], [], []
    for c in range(blocks):
        cols = slice(c * Q, (c + 1) * Q)
        step = steps[:, cols]
        logs = exact_dot(step * rates[...], prefix)
        ls_out[:, cols] = logs
        logs_held[:, cols] = logs
        end = logs[:, Q - 1 :]
        scaled = jnp.exp(end - logs) * step
        grown = jnp.exp(logs)
        xt = x[cols, :].T
        gt = g[cols, :].T
        xt_out[:, cols] = xt
        gt_out[:, cols] = gt
        xt_held[:, cols] = xt
        gt_held[:, cols] = gt
        xs, gs = [], []
        for h in range(G):
            rows = slice(h * size, (h + 1) * size)
            xs.append((xt[rows].astype(F32) * scaled[h : h + 1]).astype(BF16))
            gs.append((gt[rows].astype(F32) * grown[h : h + 1]).astype(BF16))
        fresh.append(fdot(jnp.concatenate(xs, 0), bmap[cols, :]))
        read.append(fdot(jnp.concatenate(gs, 0), cmap[cols, :]))
        ends.append(end)
    for c in range(1, blocks):
        fresh_out[c - 1] = fresh[c - 1]
        read_out[c - 1] = read[c]
    for h in range(G):
        rows = slice(h * size, (h + 1) * size)
        state = fresh[0][rows]
        cot = read[-1][rows]
        for c in range(1, blocks):
            state = jnp.exp(ends[c][h : h + 1]) * state + fresh[c][rows]
            back = blocks - 1 - c
            cot = jnp.exp(ends[back][h : h + 1]) * cot + read[back][rows]
        for k in range(n.bit_length() - 1):
            sent[k, rows, :] = jnp.where(me // 2**k % 2 == 0, state, cot)
    decay = ends[0]
    for c in range(1, blocks):
        decay = decay + ends[c]
    for k in range(n.bit_length() - 1):
        sent[k, G * size :, :] = jnp.broadcast_to(decay, (G, sent.shape[2]))


def intra_step(size, i, groups, steps, logs, g, xt, gt, bmap, cmap, gf_out, rowsum, colsum, skip,
               gin, gout, scores, total):
    blocks = steps.shape[1] // Q
    half = Q // 2

    @pl.when(i == 0)
    def _():
        row = lax.broadcasted_iota(jnp.int32, (Q, Q), 0)
        col = lax.broadcasted_iota(jnp.int32, (Q, Q), 1)
        for c in range(blocks):
            cols = slice(c * Q, (c + 1) * Q)
            s = lax.dot_general(cmap[cols, :], bmap[cols, :], NT, preferred_element_type=F32)
            scores[c] = jnp.where(row >= col, s, 0.0)
        total[...] = jnp.zeros_like(total)

    lane = lax.broadcasted_iota(jnp.int32, (Q, 2 * size), 1)
    for c in range(blocks):
        cols = slice(c * Q, (c + 1) * Q)
        base = c * Q
        lrow = logs[:, cols] * LOG2E
        lcol = lrow.T
        srow = steps[:, cols]
        acc0 = total[c, :half, :half]
        acc1 = total[c, half:, :]
        sums, col_parts, skips = [], [], []
        for h in range(G):
            pair = slice(h // 2 * 2 * size, (h // 2 + 1) * 2 * size)
            rows = slice(h * size, (h + 1) * size)
            mine = lane < size if h % 2 == 0 else lane >= size
            gm = jnp.where(mine, g[cols, pair], jnp.zeros((), BF16))
            row_parts = []
            mixes = []
            column = None
            for slab in range(2):
                ts = slice(slab * half, (slab + 1) * half)
                width = (slab + 1) * half
                ss = slice(0, width)
                inner = fdot(gm[ts], xt[pair, base : base + width])
                spread = jnp.minimum(lcol[ts, h : h + 1] - lrow[h : h + 1, ss], 0.0)
                kern = jnp.exp2(spread) * scores[c, ts, ss]
                step = srow[h : h + 1, ss]
                mixes.append((kern * step).astype(BF16))
                weighted = kern * inner
                pulled = weighted * step
                if slab == 0:
                    acc0 = acc0 + pulled
                else:
                    acc1 = acc1 + pulled
                row_parts.append(jnp.sum(pulled, axis=1, keepdims=True))
                part = jnp.sum(weighted, axis=0, keepdims=True)
                if slab == 0:
                    column = jnp.concatenate([part, jnp.zeros_like(part)], 1)
                else:
                    column = column + part
            col_parts.append(column)
            sums.append(jnp.concatenate(row_parts, 0))
            low = fdot(gt[rows, base : base + half], mixes[0])
            full = fdot(gt[rows, base + half : base + Q], mixes[1])
            gf_out[rows, base : base + half] = low + full[:, :half]
            gf_out[rows, base + half : base + Q] = full[:, half:]
            both = gt[rows, cols].astype(F32) * xt[rows, cols].astype(F32)
            skips.append(jnp.sum(both, axis=0, keepdims=True))
        total[c, :half, :half] = acc0
        total[c, half:, :] = acc1
        colsum[:, cols] = jnp.concatenate(col_parts, 0)
        rowsum[:, cols] = jnp.concatenate(sums, 1).T
        skip[:, cols] = jnp.concatenate(skips, 0)

    @pl.when(i == groups - 1)
    def _():
        for c in range(blocks):
            cols = slice(c * Q, (c + 1) * Q)
            grads = total[c].astype(BF16)
            gin[cols, :] = lax.dot_general(grads, cmap[cols, :], TN, preferred_element_type=F32)
            gout[cols, :] = fdot(grads, bmap[cols, :])


def finish_kernel(size, count, weights, gains, steps, rates, logs, rowsum, colsum, skip, xt, gt,
                  gf_in, bmap, cmap, gin, gout, first, last, fresh, read, *rest):
    received = rest[:count]
    gf, gsteps, gin_all, gout_all, rate_part, skip_part, tin, tout = rest[count:]
    i = pl.program_id(0)
    blocks = steps.shape[1] // Q
    suffix = tri("suffix")

    @pl.when(i == 0)
    def _():
        tin[...] = jnp.zeros_like(tin)
        tout[...] = jnp.zeros_like(tout)

    ends = [logs[:, (c + 1) * Q - 1 : (c + 1) * Q] for c in range(blocks)]
    entering = [[None] * G for _ in range(blocks)]
    leaving = [[None] * G for _ in range(blocks)]
    for h in range(G):
        head = i * G + h
        rows = slice(h * size, (h + 1) * size)
        state = weights[0, 0, head] * first[rows].astype(F32)
        cot = weights[1, 0, head] * last[rows].astype(F32)
        for d in range(count):
            value = received[d][0, rows]
            state = state + weights[0, d + 1, head] * value
            cot = cot + weights[1, d + 1, head] * value
        entering[0][h] = state
        leaving[-1][h] = cot
        for c in range(1, blocks):
            entering[c][h] = jnp.exp(ends[c - 1][h : h + 1]) * entering[c - 1][h] + fresh[c - 1, rows]
            b = blocks - 1 - c
            leaving[b][h] = jnp.exp(ends[b + 1][h : h + 1]) * leaving[b + 1][h] + read[b, rows]
    rate_total = jnp.zeros((G, 1), F32)
    lane = lax.broadcasted_iota(jnp.int32, (1, Q), 1)
    for c in range(blocks):
        cols = slice(c * Q, (c + 1) * Q)
        log = logs[:, cols]
        step = steps[:, cols]
        decay = jnp.exp(ends[c] - log)
        scaled = decay * step
        grown = jnp.exp(log)
        eb = jnp.concatenate([e.astype(BF16) for e in entering[c]], 0)
        lb = jnp.concatenate([e.astype(BF16) for e in leaving[c]], 0)
        out_t = lax.dot_general(eb, cmap[cols, :], NT, preferred_element_type=F32)
        in_t = lax.dot_general(lb, bmap[cols, :], NT, preferred_element_type=F32)
        xs, gs, rdots, idots, prods = [], [], [], [], []
        for h in range(G):
            rows = slice(h * size, (h + 1) * size)
            xh = xt[rows, cols].astype(F32)
            gh = gt[rows, cols].astype(F32)
            sc = scaled[h : h + 1]
            xs.append((xh * sc).astype(BF16))
            gs.append((gh * grown[h : h + 1]).astype(BF16))
            rdots.append(jnp.sum(gh * out_t[rows], axis=0, keepdims=True))
            idots.append(jnp.sum(xh * in_t[rows], axis=0, keepdims=True))
            prods.append(jnp.sum(leaving[c][h] * entering[c][h], axis=0, keepdims=True))
            grad = gf_in[rows, cols] + sc * in_t[rows] + gains[i * G + h] * gh
            gf[cols, rows] = grad.T.astype(BF16)
        tin[:, cols] += lax.dot_general(lb, jnp.concatenate(xs, 0), TN, preferred_element_type=F32)
        tout[:, cols] += lax.dot_general(eb, jnp.concatenate(gs, 0), TN, preferred_element_type=F32)
        rdot = jnp.concatenate(rdots, 0)
        idot = jnp.concatenate(idots, 0)
        prod = jnp.sum(jnp.concatenate(prods, 0), axis=1, keepdims=True)
        terms = scaled * idot
        extra = jnp.sum(terms, axis=1, keepdims=True) + jnp.exp(ends[c]) * prod
        weighted = colsum[:, cols]
        logs_grad = rowsum[:, cols] - step * weighted + grown * rdot - terms
        logs_grad = logs_grad + jnp.where(lane == Q - 1, extra, 0.0)
        through = exact_dot(logs_grad, suffix)
        gsteps[:, cols] = rates[...] * through + weighted + decay * idot
        rate_total = rate_total + jnp.sum(step * through, axis=1, keepdims=True)
    rate_part[...] = rates[...] * rate_total
    skip_part[...] = jnp.sum(skip[...], axis=1, keepdims=True)

    @pl.when(i == pl.num_programs(0) - 1)
    def _():
        gin_all[...] = gin[...] + tin[...].T
        gout_all[...] = gout[...] + tout[...].T


def sums_kernel(n, m, parts, *refs):
    rates, skips = refs[:parts], refs[parts : 2 * parts]
    out, mine, first, second, send1, recv1, send2, recv2 = refs[2 * parts :]
    here, there = lax.axis_index("ctx"), lax.axis_index("seq")
    barrier = pltpu.get_barrier_semaphore()
    for d in range(1, n):
        pl.semaphore_signal(barrier, inc=1, device_id={"ctx": lax.rem(here + d, n)},
                            device_id_type=pl.DeviceIdType.MESH)
    for d in range(1, m):
        pl.semaphore_signal(barrier, inc=1, device_id={"seq": lax.rem(there + d, m)},
                            device_id_type=pl.DeviceIdType.MESH)
    heads = out.shape[1]
    row = lax.broadcasted_iota(jnp.int32, (heads, heads), 0)
    col = lax.broadcasted_iota(jnp.int32, (heads, heads), 1)
    mine[...] = jnp.zeros_like(mine)
    for k, group in enumerate((rates, skips)):
        column = jnp.concatenate([r[...] for r in group], 0)
        line = jnp.sum(jnp.where(row == col, column, 0.0), axis=0, keepdims=True)
        mine[k : k + 1, :heads] = line
    pl.semaphore_wait(barrier, n + m - 2)

    def exchange(axis, place, count, slots, send, recv):
        copies = []
        slots[place] = mine[...]
        for d in range(1, count):
            copy = pltpu.make_async_remote_copy(
                src_ref=mine, dst_ref=slots.at[place], send_sem=send.at[d],
                recv_sem=recv.at[place], device_id={axis: lax.rem(place + d, count)},
                device_id_type=pl.DeviceIdType.MESH)
            copy.start()
            copies.append(copy)
        for d in range(1, count):
            source = lax.rem(place + count - d, count)
            pltpu.make_async_remote_copy(
                src_ref=mine, dst_ref=slots.at[source], send_sem=send.at[d],
                recv_sem=recv.at[source], device_id={axis: source},
                device_id_type=pl.DeviceIdType.MESH).wait_recv()
        for copy in copies:
            copy.wait_send()
        total = slots[0]
        for k in range(1, count):
            total = total + slots[k]
        return total

    mine[...] = exchange("ctx", here, n, first, send1, recv1)
    out[...] = exchange("seq", there, m, second, send2, recv2)[:2, :heads]


def local(features, step_sizes, rate_logs, input_map, output_map, skip_gain, state_first,
          upstream, state_last):
    heads = rate_logs.shape[0]
    length = features.shape[1]
    size = features.shape[2] // heads
    dim = input_map.shape[2]
    blocks = length // Q
    x, g, steps = features[0], upstream[0], step_sizes[0]
    bmap, cmap = input_map[0], output_map[0]
    first = state_first[0].reshape(heads * size, dim)
    last = state_last[0].reshape(heads * size, dim)
    rates = -jnp.exp(rate_logs)[:, None]
    n, m = lax.axis_size("ctx"), lax.axis_size("seq")
    me = lax.axis_index("ctx")
    levels = n.bit_length() - 1
    wide = G * size
    groups = heads // G
    params = pltpu.CompilerParams(vmem_limit_bytes=56 * 1024 * 1024)
    smem = pl.BlockSpec(memory_space=pltpu.SMEM)
    anywhere = pl.BlockSpec(memory_space=pl.ANY)
    whole = pl.BlockSpec((length, dim), lambda i: (0, 0))

    def specs():
        return (
            pl.BlockSpec((G, length), lambda i: (i, 0)),
            pl.BlockSpec((G, 1), lambda i: (i, 0)),
            pl.BlockSpec((length, wide), lambda i: (0, i)),
            pl.BlockSpec((wide, length), lambda i: (i, 0)),
            pl.BlockSpec((wide, dim), lambda i: (i, 0)),
            pl.BlockSpec((blocks - 1, wide, dim), lambda i: (0, i, 0)),
        )

    head_rows, rate_rows, natural, turned, state, inner = specs()
    row_shape = jax.ShapeDtypeStruct((heads, length), F32)
    map_shape = jax.ShapeDtypeStruct((length, dim), F32)
    turned_shape = jax.ShapeDtypeStruct((heads * size, length), BF16)

    both = pl.BlockSpec((G, length), lambda i: (lax.rem(i, groups), 0))
    both_rates = pl.BlockSpec((G, 1), lambda i: (lax.rem(i, groups), 0))
    both_natural = pl.BlockSpec((length, wide), lambda i: (0, lax.rem(i, groups)))
    early_natural = pl.BlockSpec((length, wide), lambda i: (0, jnp.minimum(i, groups - 1)))
    early_rows = pl.BlockSpec((G, length), lambda i: (jnp.minimum(i, groups - 1), 0))
    early_turned = pl.BlockSpec((wide, length), lambda i: (jnp.minimum(i, groups - 1), 0))
    early_inner = pl.BlockSpec((blocks - 1, wide, dim), lambda i: (0, jnp.minimum(i, groups - 1), 0))
    late_turned = pl.BlockSpec((wide, length), lambda i: (jnp.maximum(i - groups, 0), 0))
    late_rows = pl.BlockSpec((G, length), lambda i: (jnp.maximum(i - groups, 0), 0))
    inner_shape = jax.ShapeDtypeStruct((blocks - 1, heads * size, dim), F32)
    message = jax.ShapeDtypeStruct((groups, wide + G, dim), F32)
    (logs, xt, gt, fresh, read, gf_in, rowsum, colsum, skip, gin, gout, *received) = pl.pallas_call(
        partial(local_kernel, size, n),
        grid=(2 * groups,),
        in_specs=[both, both_rates, early_natural, both_natural, whole, whole],
        out_specs=[early_rows, early_turned, early_turned, early_inner, early_inner,
                   late_turned, late_rows, late_rows, late_rows, whole, whole]
        + [anywhere] * (n - 1),
        out_shape=[row_shape, turned_shape, turned_shape, inner_shape, inner_shape,
                   jax.ShapeDtypeStruct((heads * size, length), F32), row_shape, row_shape,
                   row_shape, map_shape, map_shape] + [message] * (n - 1),
        scratch_shapes=[pltpu.VMEM((blocks, Q, Q), F32)] * 2
        + [pltpu.VMEM((groups, G, length), F32)]
        + [pltpu.VMEM((groups, wide, length), BF16)] * 2
        + [pltpu.VMEM((groups, levels, wide + G, dim), F32),
           pltpu.SemaphoreType.DMA((n - 1, groups)), pltpu.SemaphoreType.DMA((n - 1, groups))],
        compiler_params=pltpu.CompilerParams(vmem_limit_bytes=56 * 1024 * 1024, collective_id=1,
                                             has_side_effects=True),
        name="local_grads",
        cost_estimate=pl.CostEstimate(flops=2 * 10**10, bytes_accessed=30 * 10**6,
                                      transcendentals=0),
    )(steps, rates, x, g, bmap, cmap)

    others = jnp.arange(n)
    esum = logs[:, Q - 1 :: Q].sum(1)
    by_distance = jnp.stack([esum] + [r[:, wide:, 0].reshape(heads) for r in received])
    by_place = by_distance[others ^ me]
    source = (me ^ others)[:, None]
    between = others[None, :]
    ahead = (source < between) & (between < me)
    behind = (me < between) & (between < source)
    fore = jnp.where(source < me, jnp.exp(jnp.where(ahead[:, :, None], by_place[None], 0.0).sum(1)), 0.0)
    aft = jnp.where(source > me, jnp.exp(jnp.where(behind[:, :, None], by_place[None], 0.0).sum(1)), 0.0)
    enter = jnp.exp(jnp.where((others < me)[:, None], by_place, 0.0).sum(0))
    leave = jnp.exp(jnp.where((others > me)[:, None], by_place, 0.0).sum(0))
    weights = jnp.stack([fore.at[0].set(enter), aft.at[0].set(leave)])

    one_shape = jax.ShapeDtypeStruct((heads, 1), F32)
    arrived = pl.BlockSpec((1, wide + G, dim), lambda i: (i, 0, 0))
    gf, gsteps, gin, gout, rate_part, skip_part = pl.pallas_call(
        partial(finish_kernel, size, n - 1),
        grid=(groups,),
        in_specs=[smem, smem, head_rows, rate_rows, head_rows, head_rows, head_rows,
                  head_rows, turned, turned, turned, whole, whole, whole, whole, state, state,
                  inner, inner] + [arrived] * (n - 1),
        out_specs=[natural, head_rows, whole, whole, rate_rows, rate_rows],
        out_shape=[jax.ShapeDtypeStruct((length, heads * size), BF16), row_shape, map_shape,
                   map_shape, one_shape, one_shape],
        scratch_shapes=[pltpu.VMEM((dim, length), F32)] * 2,
        compiler_params=params,
        name="finish",
        cost_estimate=pl.CostEstimate(flops=2 * 10**9, bytes_accessed=30 * 10**6,
                                      transcendentals=0),
    )(weights, skip_gain, steps, rates, logs, rowsum, colsum, skip, xt, gt, gf_in, bmap, cmap,
      gin, gout, first, last, fresh, read, *received)

    lanes = -(-heads // 128) * 128
    vmem = pl.BlockSpec(memory_space=pltpu.VMEM)
    dma = pltpu.SemaphoreType.DMA
    totals = pl.pallas_call(
        partial(sums_kernel, n, m, 1),
        in_specs=[vmem] * 2,
        out_specs=vmem,
        out_shape=jax.ShapeDtypeStruct((2, heads), F32),
        scratch_shapes=[pltpu.VMEM((8, lanes), F32), pltpu.VMEM((n, 8, lanes), F32),
                        pltpu.VMEM((m, 8, lanes), F32), dma((n,)), dma((n,)), dma((m,)),
                        dma((m,))],
        compiler_params=pltpu.CompilerParams(collective_id=0, has_side_effects=True),
        name="sums",
    )(rate_part, skip_part)
    return (gf[None], gsteps[None], gin[None], gout[None], totals[0], totals[1])


def solution(mesh):
    tokens = P("seq", "ctx", None)
    state = P("seq", None, None, None)
    head_tokens = P("seq", None, "ctx")
    return jax.shard_map(
        local,
        mesh=mesh,
        in_specs=(tokens, head_tokens, P(), tokens, tokens, P(), state, tokens, state),
        out_specs=(tokens, head_tokens, tokens, tokens, P(), P()),
        check_vma=False,
    )
```

```python
from functools import partial

import jax
import jax.numpy as jnp
from jax import lax
from jax.experimental import pallas as pl
from jax.experimental.pallas import tpu as pltpu
from jax.sharding import PartitionSpec as P

Q = 256
G = 8
LOG2E = 1.4426950408889634
F32 = jnp.float32
BF16 = jnp.bfloat16
NT = (((1,), (1,)), ((), ()))
TN = (((0,), (0,)), ((), ()))


def fdot(a, b):
    return jnp.dot(a, b, preferred_element_type=F32)


def exact_dot(a, b):
    return jnp.dot(a, b, preferred_element_type=F32, precision=lax.Precision.HIGHEST)


def tri(kind):
    row = lax.broadcasted_iota(jnp.int32, (Q, Q), 0)
    col = lax.broadcasted_iota(jnp.int32, (Q, Q), 1)
    return (row <= col if kind == "prefix" else row >= col).astype(F32)


def partner(place, distance):
    other = place
    for k in range(distance.bit_length()):
        if distance >> k & 1:
            other = other + (1 - 2 * (place // 2**k % 2)) * 2**k
    return other


def local_kernel(size, n, steps, rates, x, g, bmap, cmap, *refs):
    ls_out, xt_out, gt_out, fresh_out, read_out = refs[:5]
    gf_out, rowsum, colsum, skip, gin, gout = refs[5:11]
    received, scores, total, logs, xts, gts, sent, send_sem, recv_sem = refs[11:]
    i = pl.program_id(0)
    groups = pl.num_programs(0) // 2
    me = lax.axis_index("ctx")

    def copy(d, group):
        return pltpu.make_async_remote_copy(
            src_ref=sent.at[group, d.bit_length() - 1], dst_ref=received.at[d - 1, group],
            send_sem=send_sem.at[d - 1, group], recv_sem=recv_sem.at[d - 1, group],
            device_id={"ctx": partner(me, d)}, device_id_type=pl.DeviceIdType.MESH)

    @pl.when(i == 0)
    def _():
        barrier = pltpu.get_barrier_semaphore()
        for d in range(1, n):
            pl.semaphore_signal(barrier, inc=1, device_id={"ctx": partner(me, d)},
                                device_id_type=pl.DeviceIdType.MESH)
        pl.semaphore_wait(barrier, n - 1)

    @pl.when(i < groups)
    def _():
        states_step(size, n, me, steps, rates, x, g, bmap, cmap, ls_out, xt_out, gt_out,
                    fresh_out, read_out, logs.at[i], xts.at[i], gts.at[i], sent.at[i])
        for d in range(1, n):
            copy(d, i).start()

    @pl.when(i >= groups)
    def _():
        k = i - groups
        intra_step(size, k, groups, steps, logs.at[k], g, xts.at[k], gts.at[k], bmap, cmap,
                   gf_out, rowsum, colsum, skip, gin, gout, scores, total)

    @pl.when(i == 2 * groups - 1)
    def _():
        for group in range(sent.shape[0]):
            for d in range(1, n):
                copy(d, group).wait()


def states_step(size, n, me, steps, rates, x, g, bmap, cmap, ls_out, xt_out, gt_out, fresh_out,
                read_out, logs_held, xt_held, gt_held, sent):
    blocks = steps.shape[1] // Q
    prefix = tri("prefix")
    fresh, read, ends = [], [], []
    for c in range(blocks):
        cols = slice(c * Q, (c + 1) * Q)
        step = steps[:, cols]
        logs = exact_dot(step * rates[...], prefix)
        ls_out[:, cols] = logs
        logs_held[:, cols] = logs
        end = logs[:, Q - 1 :]
        scaled = jnp.exp(end - logs) * step
        grown = jnp.exp(logs)
        xt = x[cols, :].T
        gt = g[cols, :].T
        xt_out[:, cols] = xt
        gt_out[:, cols] = gt
        xt_held[:, cols] = xt
        gt_held[:, cols] = gt
        xs, gs = [], []
        for h in range(G):
            rows = slice(h * size, (h + 1) * size)
            xs.append((xt[rows].astype(F32) * scaled[h : h + 1]).astype(BF16))
            gs.append((gt[rows].astype(F32) * grown[h : h + 1]).astype(BF16))
        fresh.append(fdot(jnp.concatenate(xs, 0), bmap[cols, :]))
        read.append(fdot(jnp.concatenate(gs, 0), cmap[cols, :]))
        ends.append(end)
    for c in range(1, blocks):
        fresh_out[c - 1] = fresh[c - 1]
        read_out[c - 1] = read[c]
    for h in range(G):
        rows = slice(h * size, (h + 1) * size)
        state = fresh[0][rows]
        cot = read[-1][rows]
        for c in range(1, blocks):
            state = jnp.exp(ends[c][h : h + 1]) * state + fresh[c][rows]
            back = blocks - 1 - c
            cot = jnp.exp(ends[back][h : h + 1]) * cot + read[back][rows]
        for k in range(n.bit_length() - 1):
            sent[k, rows, :] = jnp.where(me // 2**k % 2 == 0, state, cot)
    decay = ends[0]
    for c in range(1, blocks):
        decay = decay + ends[c]
    for k in range(n.bit_length() - 1):
        sent[k, G * size :, :] = jnp.broadcast_to(decay, (G, sent.shape[2]))


def intra_step(size, i, groups, steps, logs, g, xt, gt, bmap, cmap, gf_out, rowsum, colsum, skip,
               gin, gout, scores, total):
    blocks = steps.shape[1] // Q
    half = Q // 2

    @pl.when(i == 0)
    def _():
        row = lax.broadcasted_iota(jnp.int32, (Q, Q), 0)
        col = lax.broadcasted_iota(jnp.int32, (Q, Q), 1)
        for c in range(blocks):
            cols = slice(c * Q, (c + 1) * Q)
            s = lax.dot_general(cmap[cols, :], bmap[cols, :], NT, preferred_element_type=F32)
            scores[c] = jnp.where(row >= col, s, 0.0)
        total[...] = jnp.zeros_like(total)

    lane = lax.broadcasted_iota(jnp.int32, (Q, 2 * size), 1)
    for c in range(blocks):
        cols = slice(c * Q, (c + 1) * Q)
        base = c * Q
        lrow = logs[:, cols] * LOG2E
        lcol = lrow.T
        srow = steps[:, cols]
        acc0 = total[c, :half, :half]
        acc1 = total[c, half:, :]
        sums, col_parts, skips = [], [], []
        for h in range(G):
            pair = slice(h // 2 * 2 * size, (h // 2 + 1) * 2 * size)
            rows = slice(h * size, (h + 1) * size)
            mine = lane < size if h % 2 == 0 else lane >= size
            gm = jnp.where(mine, g[cols, pair], jnp.zeros((), BF16))
            row_parts = []
            mixes = []
            column = None
            for slab in range(2):
                ts = slice(slab * half, (slab + 1) * half)
                width = (slab + 1) * half
                ss = slice(0, width)
                inner = fdot(gm[ts], xt[pair, base : base + width])
                spread = jnp.minimum(lcol[ts, h : h + 1] - lrow[h : h + 1, ss], 0.0)
                kern = jnp.exp2(spread) * scores[c, ts, ss]
                step = srow[h : h + 1, ss]
                mixes.append((kern * step).astype(BF16))
                weighted = kern * inner
                pulled = weighted * step
                if slab == 0:
                    acc0 = acc0 + pulled
                else:
                    acc1 = acc1 + pulled
                row_parts.append(jnp.sum(pulled, axis=1, keepdims=True))
                part = jnp.sum(weighted, axis=0, keepdims=True)
                if slab == 0:
                    column = jnp.concatenate([part, jnp.zeros_like(part)], 1)
                else:
                    column = column + part
            col_parts.append(column)
            sums.append(jnp.concatenate(row_parts, 0))
            low = fdot(gt[rows, base : base + half], mixes[0])
            full = fdot(gt[rows, base + half : base + Q], mixes[1])
            gf_out[rows, base : base + half] = low + full[:, :half]
            gf_out[rows, base + half : base + Q] = full[:, half:]
            both = gt[rows, cols].astype(F32) * xt[rows, cols].astype(F32)
            skips.append(jnp.sum(both, axis=0, keepdims=True))
        total[c, :half, :half] = acc0
        total[c, half:, :] = acc1
        colsum[:, cols] = jnp.concatenate(col_parts, 0)
        rowsum[:, cols] = jnp.concatenate(sums, 1).T
        skip[:, cols] = jnp.concatenate(skips, 0)

    @pl.when(i == groups - 1)
    def _():
        for c in range(blocks):
            cols = slice(c * Q, (c + 1) * Q)
            grads = total[c].astype(BF16)
            gin[cols, :] = lax.dot_general(grads, cmap[cols, :], TN, preferred_element_type=F32)
            gout[cols, :] = fdot(grads, bmap[cols, :])


def finish_kernel(size, count, weights, gains, steps, rates, logs, rowsum, colsum, skip, xt, gt,
                  gf_in, bmap, cmap, gin, gout, first, last, fresh, read, *rest):
    received = rest[:count]
    gf, gsteps, gin_all, gout_all, rate_part, skip_part, tin, tout = rest[count:]
    i = pl.program_id(0)
    blocks = steps.shape[1] // Q
    suffix = tri("suffix")

    @pl.when(i == 0)
    def _():
        tin[...] = jnp.zeros_like(tin)
        tout[...] = jnp.zeros_like(tout)

    ends = [logs[:, (c + 1) * Q - 1 : (c + 1) * Q] for c in range(blocks)]
    entering = [[None] * G for _ in range(blocks)]
    leaving = [[None] * G for _ in range(blocks)]
    for h in range(G):
        head = i * G + h
        rows = slice(h * size, (h + 1) * size)
        state = weights[0, 0, head] * first[rows].astype(F32)
        cot = weights[1, 0, head] * last[rows].astype(F32)
        for d in range(count):
            value = received[d][0, 0, rows]
            state = state + weights[0, d + 1, head] * value
            cot = cot + weights[1, d + 1, head] * value
        entering[0][h] = state
        leaving[-1][h] = cot
        for c in range(1, blocks):
            entering[c][h] = jnp.exp(ends[c - 1][h : h + 1]) * entering[c - 1][h] + fresh[c - 1, rows]
            b = blocks - 1 - c
            leaving[b][h] = jnp.exp(ends[b + 1][h : h + 1]) * leaving[b + 1][h] + read[b, rows]
    rate_total = jnp.zeros((G, 1), F32)
    lane = lax.broadcasted_iota(jnp.int32, (1, Q), 1)
    for c in range(blocks):
        cols = slice(c * Q, (c + 1) * Q)
        log = logs[:, cols]
        step = steps[:, cols]
        decay = jnp.exp(ends[c] - log)
        scaled = decay * step
        grown = jnp.exp(log)
        eb = jnp.concatenate([e.astype(BF16) for e in entering[c]], 0)
        lb = jnp.concatenate([e.astype(BF16) for e in leaving[c]], 0)
        out_t = lax.dot_general(eb, cmap[cols, :], NT, preferred_element_type=F32)
        in_t = lax.dot_general(lb, bmap[cols, :], NT, preferred_element_type=F32)
        xs, gs, rdots, idots, prods = [], [], [], [], []
        for h in range(G):
            rows = slice(h * size, (h + 1) * size)
            xh = xt[rows, cols].astype(F32)
            gh = gt[rows, cols].astype(F32)
            sc = scaled[h : h + 1]
            xs.append((xh * sc).astype(BF16))
            gs.append((gh * grown[h : h + 1]).astype(BF16))
            rdots.append(jnp.sum(gh * out_t[rows], axis=0, keepdims=True))
            idots.append(jnp.sum(xh * in_t[rows], axis=0, keepdims=True))
            prods.append(jnp.sum(leaving[c][h] * entering[c][h], axis=0, keepdims=True))
            grad = gf_in[rows, cols] + sc * in_t[rows] + gains[i * G + h] * gh
            gf[cols, rows] = grad.T.astype(BF16)
        tin[:, cols] += lax.dot_general(lb, jnp.concatenate(xs, 0), TN, preferred_element_type=F32)
        tout[:, cols] += lax.dot_general(eb, jnp.concatenate(gs, 0), TN, preferred_element_type=F32)
        rdot = jnp.concatenate(rdots, 0)
        idot = jnp.concatenate(idots, 0)
        prod = jnp.sum(jnp.concatenate(prods, 0), axis=1, keepdims=True)
        terms = scaled * idot
        extra = jnp.sum(terms, axis=1, keepdims=True) + jnp.exp(ends[c]) * prod
        weighted = colsum[:, cols]
        logs_grad = rowsum[:, cols] - step * weighted + grown * rdot - terms
        logs_grad = logs_grad + jnp.where(lane == Q - 1, extra, 0.0)
        through = exact_dot(logs_grad, suffix)
        gsteps[:, cols] = rates[...] * through + weighted + decay * idot
        rate_total = rate_total + jnp.sum(step * through, axis=1, keepdims=True)
    rate_part[...] = rates[...] * rate_total
    skip_part[...] = jnp.sum(skip[...], axis=1, keepdims=True)

    @pl.when(i == pl.num_programs(0) - 1)
    def _():
        gin_all[...] = gin[...] + tin[...].T
        gout_all[...] = gout[...] + tout[...].T


def sums_kernel(n, m, parts, *refs):
    rates, skips = refs[:parts], refs[parts : 2 * parts]
    out, mine, first, second, send1, recv1, send2, recv2 = refs[2 * parts :]
    here, there = lax.axis_index("ctx"), lax.axis_index("seq")
    barrier = pltpu.get_barrier_semaphore()
    for d in range(1, n):
        pl.semaphore_signal(barrier, inc=1, device_id={"ctx": lax.rem(here + d, n)},
                            device_id_type=pl.DeviceIdType.MESH)
    for d in range(1, m):
        pl.semaphore_signal(barrier, inc=1, device_id={"seq": lax.rem(there + d, m)},
                            device_id_type=pl.DeviceIdType.MESH)
    heads = out.shape[1]
    row = lax.broadcasted_iota(jnp.int32, (heads, heads), 0)
    col = lax.broadcasted_iota(jnp.int32, (heads, heads), 1)
    mine[...] = jnp.zeros_like(mine)
    for k, group in enumerate((rates, skips)):
        column = jnp.concatenate([r[...] for r in group], 0)
        line = jnp.sum(jnp.where(row == col, column, 0.0), axis=0, keepdims=True)
        mine[k : k + 1, :heads] = line
    pl.semaphore_wait(barrier, n + m - 2)

    def exchange(axis, place, count, slots, send, recv):
        copies = []
        slots[place] = mine[...]
        for d in range(1, count):
            copy = pltpu.make_async_remote_copy(
                src_ref=mine, dst_ref=slots.at[place], send_sem=send.at[d],
                recv_sem=recv.at[place], device_id={axis: lax.rem(place + d, count)},
                device_id_type=pl.DeviceIdType.MESH)
            copy.start()
            copies.append(copy)
        for d in range(1, count):
            source = lax.rem(place + count - d, count)
            pltpu.make_async_remote_copy(
                src_ref=mine, dst_ref=slots.at[source], send_sem=send.at[d],
                recv_sem=recv.at[source], device_id={axis: source},
                device_id_type=pl.DeviceIdType.MESH).wait_recv()
        for copy in copies:
            copy.wait_send()
        total = slots[0]
        for k in range(1, count):
            total = total + slots[k]
        return total

    mine[...] = exchange("ctx", here, n, first, send1, recv1)
    out[...] = exchange("seq", there, m, second, send2, recv2)[:2, :heads]


def local(features, step_sizes, rate_logs, input_map, output_map, skip_gain, state_first,
          upstream, state_last):
    heads = rate_logs.shape[0]
    length = features.shape[1]
    size = features.shape[2] // heads
    dim = input_map.shape[2]
    blocks = length // Q
    x, g, steps = features[0], upstream[0], step_sizes[0]
    bmap, cmap = input_map[0], output_map[0]
    first = state_first[0].reshape(heads * size, dim)
    last = state_last[0].reshape(heads * size, dim)
    rates = -jnp.exp(rate_logs)[:, None]
    n, m = lax.axis_size("ctx"), lax.axis_size("seq")
    me = lax.axis_index("ctx")
    levels = n.bit_length() - 1
    wide = G * size
    groups = heads // G
    params = pltpu.CompilerParams(vmem_limit_bytes=56 * 1024 * 1024)
    smem = pl.BlockSpec(memory_space=pltpu.SMEM)
    anywhere = pl.BlockSpec(memory_space=pl.ANY)
    whole = pl.BlockSpec((length, dim), lambda i: (0, 0))

    def specs():
        return (
            pl.BlockSpec((G, length), lambda i: (i, 0)),
            pl.BlockSpec((G, 1), lambda i: (i, 0)),
            pl.BlockSpec((length, wide), lambda i: (0, i)),
            pl.BlockSpec((wide, length), lambda i: (i, 0)),
            pl.BlockSpec((wide, dim), lambda i: (i, 0)),
            pl.BlockSpec((blocks - 1, wide, dim), lambda i: (0, i, 0)),
        )

    head_rows, rate_rows, natural, turned, state, inner = specs()
    row_shape = jax.ShapeDtypeStruct((heads, length), F32)
    map_shape = jax.ShapeDtypeStruct((length, dim), F32)
    turned_shape = jax.ShapeDtypeStruct((heads * size, length), BF16)

    both = pl.BlockSpec((G, length), lambda i: (lax.rem(i, groups), 0))
    both_rates = pl.BlockSpec((G, 1), lambda i: (lax.rem(i, groups), 0))
    both_natural = pl.BlockSpec((length, wide), lambda i: (0, lax.rem(i, groups)))
    early_natural = pl.BlockSpec((length, wide), lambda i: (0, jnp.minimum(i, groups - 1)))
    early_rows = pl.BlockSpec((G, length), lambda i: (jnp.minimum(i, groups - 1), 0))
    early_turned = pl.BlockSpec((wide, length), lambda i: (jnp.minimum(i, groups - 1), 0))
    early_inner = pl.BlockSpec((blocks - 1, wide, dim), lambda i: (0, jnp.minimum(i, groups - 1), 0))
    late_turned = pl.BlockSpec((wide, length), lambda i: (jnp.maximum(i - groups, 0), 0))
    late_rows = pl.BlockSpec((G, length), lambda i: (jnp.maximum(i - groups, 0), 0))
    inner_shape = jax.ShapeDtypeStruct((blocks - 1, heads * size, dim), F32)
    message = jax.ShapeDtypeStruct((n - 1, groups, wide + G, dim), F32)
    (logs, xt, gt, fresh, read, gf_in, rowsum, colsum, skip, gin, gout, received) = pl.pallas_call(
        partial(local_kernel, size, n),
        grid=(2 * groups,),
        in_specs=[both, both_rates, early_natural, both_natural, whole, whole],
        out_specs=[early_rows, early_turned, early_turned, early_inner, early_inner,
                   late_turned, late_rows, late_rows, late_rows, whole, whole]
        + [anywhere],
        out_shape=[row_shape, turned_shape, turned_shape, inner_shape, inner_shape,
                   jax.ShapeDtypeStruct((heads * size, length), F32), row_shape, row_shape,
                   row_shape, map_shape, map_shape, message],
        scratch_shapes=[pltpu.VMEM((blocks, Q, Q), F32)] * 2
        + [pltpu.VMEM((groups, G, length), F32)]
        + [pltpu.VMEM((groups, wide, length), BF16)] * 2
        + [pltpu.VMEM((groups, levels, wide + G, dim), F32),
           pltpu.SemaphoreType.DMA((n - 1, groups)), pltpu.SemaphoreType.DMA((n - 1, groups))],
        compiler_params=pltpu.CompilerParams(vmem_limit_bytes=56 * 1024 * 1024, collective_id=1,
                                             has_side_effects=True),
        name="local_grads",
        cost_estimate=pl.CostEstimate(flops=2 * 10**10, bytes_accessed=30 * 10**6,
                                      transcendentals=0),
    )(steps, rates, x, g, bmap, cmap)

    others = jnp.arange(n)
    esum = logs[:, Q - 1 :: Q].sum(1)
    by_distance = jnp.concatenate([esum[None], received[:, :, wide:, 0].reshape(n - 1, heads)])
    by_place = by_distance[others ^ me]
    source = (me ^ others)[:, None]
    between = others[None, :]
    ahead = (source < between) & (between < me)
    behind = (me < between) & (between < source)
    fore = jnp.where(source < me, jnp.exp(jnp.where(ahead[:, :, None], by_place[None], 0.0).sum(1)), 0.0)
    aft = jnp.where(source > me, jnp.exp(jnp.where(behind[:, :, None], by_place[None], 0.0).sum(1)), 0.0)
    enter = jnp.exp(jnp.where((others < me)[:, None], by_place, 0.0).sum(0))
    leave = jnp.exp(jnp.where((others > me)[:, None], by_place, 0.0).sum(0))
    weights = jnp.stack([fore.at[0].set(enter), aft.at[0].set(leave)])

    one_shape = jax.ShapeDtypeStruct((heads, 1), F32)
    arrived = [pl.BlockSpec((1, 1, wide + G, dim), lambda i, d=d: (d, i, 0, 0)) for d in range(n - 1)]
    gf, gsteps, gin, gout, rate_part, skip_part = pl.pallas_call(
        partial(finish_kernel, size, n - 1),
        grid=(groups,),
        in_specs=[smem, smem, head_rows, rate_rows, head_rows, head_rows, head_rows,
                  head_rows, turned, turned, turned, whole, whole, whole, whole, state, state,
                  inner, inner] + arrived,
        out_specs=[natural, head_rows, whole, whole, rate_rows, rate_rows],
        out_shape=[jax.ShapeDtypeStruct((length, heads * size), BF16), row_shape, map_shape,
                   map_shape, one_shape, one_shape],
        scratch_shapes=[pltpu.VMEM((dim, length), F32)] * 2,
        compiler_params=params,
        name="finish",
        cost_estimate=pl.CostEstimate(flops=2 * 10**9, bytes_accessed=30 * 10**6,
                                      transcendentals=0),
    )(weights, skip_gain, steps, rates, logs, rowsum, colsum, skip, xt, gt, gf_in, bmap, cmap,
      gin, gout, first, last, fresh, read, *[received] * (n - 1))

    lanes = -(-heads // 128) * 128
    vmem = pl.BlockSpec(memory_space=pltpu.VMEM)
    dma = pltpu.SemaphoreType.DMA
    totals = pl.pallas_call(
        partial(sums_kernel, n, m, 1),
        in_specs=[vmem] * 2,
        out_specs=vmem,
        out_shape=jax.ShapeDtypeStruct((2, heads), F32),
        scratch_shapes=[pltpu.VMEM((8, lanes), F32), pltpu.VMEM((n, 8, lanes), F32),
                        pltpu.VMEM((m, 8, lanes), F32), dma((n,)), dma((n,)), dma((m,)),
                        dma((m,))],
        compiler_params=pltpu.CompilerParams(collective_id=0, has_side_effects=True),
        name="sums",
    )(rate_part, skip_part)
    return (gf[None], gsteps[None], gin[None], gout[None], totals[0], totals[1])


def solution(mesh):
    tokens = P("seq", "ctx", None)
    state = P("seq", None, None, None)
    head_tokens = P("seq", None, "ctx")
    return jax.shard_map(
        local,
        mesh=mesh,
        in_specs=(tokens, head_tokens, P(), tokens, tokens, P(), state, tokens, state),
        out_specs=(tokens, head_tokens, tokens, tokens, P(), P()),
        check_vma=False,
    )
```
